256 devices in a mesh: island: 8 (over z), fsdp: 8 (over y, x_hi), dp: 4 (over x_lo, core).
Axes of the slice: x: 4 (x_hi: 2, x_lo: 2; x = x_hi * 2 + x_lo), y: 4, z: 8, core: 2. Of those that a mesh axis runs over, the one named last changes fastest.
Arguments:
- tokens: bfloat16 [196608, 4096], P(('island', 'fsdp', 'dp')), may hold values from -24 to 24
- targets: bfloat16 [196608, 1024], P(('island', 'fsdp', 'dp')), may hold values from -6 to 6
- kv_weight: float32 [4096, 1024], P(('fsdp', 'dp')), may hold values from -6 to 6
- momentum: float32 [4096, 1024], P(('fsdp', 'dp')), may hold values from -1.5 to 1.5
- first_moment: float32 [8, 4096, 1024], P('island', ('fsdp', 'dp')), may hold values from -4 to 4
- second_moment: float32 [8, 4096, 1024], P('island', ('fsdp', 'dp')), may hold values from 0.05 to 2
- step: int32 [], replicated, may hold values from 1 to 63
Outputs:
- new_weight: float32 [4096, 1024], P(('fsdp', 'dp'))
- new_momentum: float32 [4096, 1024], P(('fsdp', 'dp'))
- new_first: float32 [8, 4096, 1024], P('island', ('fsdp', 'dp'))
- new_second: float32 [8, 4096, 1024], P('island', ('fsdp', 'dp'))
The draws below stay inside these ranges and needn't reach their ends.
All inputs are finite; a program needn't handle non-finite values.
Results may differ from the reference program's by a relative error of at most 0.024.
Values may be sent and summed in bfloat16 or wider, within the bound.
No kernel may reach another device: no remote copies, remote signals or barrier semaphores. Data moves between devices by JAX's collectives and lax.ppermute only.
A program may use at most 128 MiB of HBM per device.

```python
import math
import jax
import jax.numpy as jnp
from jax import lax

D = 4096
WARM = 32
TOK_DEV = 768
KV2 = 1024
ISL_TOK = 24576
TOKENS = 196608
N_ISLAND = 8
N_FSDP = 8
N_DP = 4


def raised(entries, rng, source, target, blocks, factor):
    def block_of(dim):
        return (jnp.arange(entries.shape[dim]) // (entries.shape[dim] // blocks)).reshape((-1,) + (1,) * (entries.ndim - 1 - dim))

    near = jax.random.permutation(rng, blocks)[block_of(target)]
    far = (block_of(target) + blocks // 2) % blocks
    return jnp.where((block_of(source) == near) | (block_of(source) == far), factor * entries, entries)


def level_of(own_key, shape, split, least, largest):
    level = 1.0
    for axis_at, shards_of in split:
        steps = jax.random.uniform(jax.random.fold_in(jax.random.fold_in(own_key, 6), axis_at), (shards_of,), jnp.float32, least / len(split), largest / len(split))
        level = level * jnp.repeat(jnp.exp(steps), shape[axis_at] // shards_of).reshape((-1,) + (1,) * (len(shape) - 1 - axis_at))
    return level


def noise(rng, shape, deviation, bound, split=(), dtype=jnp.bfloat16):
    drawn = jax.random.normal(rng, shape, jnp.float32) * deviation
    if len(split) > 0:
        drawn = level_of(rng, shape, split, -0.22, 0.18) * drawn
    return jnp.clip(drawn, min=-bound, max=bound).astype(dtype)


def noise_with(key, shape, scale, reach, cuts, heavy, held_as=jnp.bfloat16):
    values = scale * jax.random.normal(key, shape, jnp.float32)
    if cuts:
        values = values * level_of(key, shape, cuts, -0.22, 0.18)
    return jnp.clip(raised(values, jax.random.fold_in(key, 3), *heavy), -reach, reach).astype(held_as)


def setup_inputs(seed: int = 0) -> dict:
    splits = jax.random.split(jax.random.key(seed), 8)
    return {
        "tokens": noise_with(splits[0], (TOKENS, D), 1.0, 24.0, ((0, 256),), (0, 1, 256, 6.0)),
        "targets": noise(splits[1], (TOKENS, KV2), 1.0, 6.0, ((0, 256),)),
        "kv_weight": noise(splits[2], (D, KV2), 1.0, 6.0, ((0, 32),), jnp.float32),
        "momentum": noise(splits[3], (D, KV2), 0.1, 1.5, ((0, 32),), jnp.float32),
        "first_moment": noise(splits[4], (N_ISLAND, D, KV2), 0.3, 4.0, ((0, 8), (1, 32)), jnp.float32),
        "second_moment": jnp.clip(jnp.exp(math.log(2.0) - 3.6888794 * jax.random.uniform(splits[5], (N_ISLAND, D, KV2), jnp.float32) ** level_of(splits[5], (N_ISLAND, D, KV2), ((0, 8), (1, 32)), -0.2, 0.2)), 0.05, 2.0),
        "step": jax.random.randint(splits[6], (), 1, 64).astype(jnp.int32),
    }


def island_step(weight_half, weight, block_tokens, block_targets, first, second, step):
    inv_width = 1.0 / jnp.sqrt(jnp.float32(D))
    inv_count = 1.0 / jnp.sqrt(jnp.float32(ISL_TOK))

    def add_block(total, pair):
        rows, goals = pair
        proj = jnp.dot(rows, weight_half, preferred_element_type=jnp.float32)
        scaled = ((proj * inv_width - goals.astype(jnp.float32)) * inv_count).astype(jnp.bfloat16)
        term = lax.dot_general(rows, scaled, (((0,), (0,)), ((), ())), preferred_element_type=jnp.float32)
        term = lax.optimization_barrier(term.astype(jnp.bfloat16)).astype(jnp.float32)
        return (total + term, None)
    start = jnp.zeros((D, KV2), jnp.float32)
    grad, unused = lax.scan(add_block, start, (block_tokens, block_targets))
    new_first = 0.9 * first + 0.1 * grad
    new_second = 0.95 * second + 0.05 * grad * grad
    count = step.astype(jnp.float32)
    rate = 0.1 * jnp.minimum(count, jnp.float32(WARM)) / jnp.float32(WARM)
    first_hat = new_first / (1.0 - jnp.power(jnp.float32(0.9), count))
    second_hat = new_second / (1.0 - jnp.power(jnp.float32(0.95), count))
    update = first_hat / (jnp.sqrt(second_hat) + 1e-08)
    pseudo = rate * (update + 0.1 * weight)
    return (new_first, new_second, pseudo)

def reference(tokens, targets, kv_weight, momentum, first_moment, second_moment, step):
    group = N_FSDP * N_DP
    weight_half = kv_weight.astype(jnp.bfloat16)
    all_tokens = tokens.reshape(N_ISLAND, group, TOK_DEV, D)
    all_targets = targets.reshape(N_ISLAND, group, TOK_DEV, KV2)

    def one_island(items):
        block_tokens, block_targets, first, second = items
        return island_step(weight_half, kv_weight, block_tokens, block_targets, first, second, step)
    new_first, new_second, pseudo = lax.map(one_island, (all_tokens, all_targets, first_moment, second_moment))
    mean_pseudo = lax.optimization_barrier(jnp.sum(pseudo, axis=0)) / jnp.float32(N_ISLAND)
    new_momentum = 0.9 * momentum + mean_pseudo
    new_weight = kv_weight - 0.7 * (mean_pseudo + 0.9 * new_momentum)
    return (new_weight, new_momentum, new_first, new_second)
```

```python
import functools
import jax
import jax.numpy as jnp
from jax import lax
from jax.experimental import pallas as pl
from jax.experimental.pallas import tpu as pltpu
from jax.sharding import PartitionSpec as P

WARM = 32
NX = NY = 4
NZ = 8
NC = 1
AXES = ("island", "fsdp", "dp")
MIB = 1024 * 1024
VM = pl.BlockSpec(memory_space=pltpu.VMEM)
SM = pl.BlockSpec(memory_space=pltpu.SMEM)


def flat(z, y, x, c):
    return (z % NZ) * 32 + (y % NY) * 8 + (x % NX) * 2 + c


def send(value, where):
    pairs = [
        (flat(z, y, x, c), flat(*where(z, y, x, c)))
        for z in range(NZ)
        for y in range(NY)
        for x in range(NX)
        for c in range(2)
    ]
    return lax.ppermute(value, AXES, pairs)


def near(k):
    return lambda z, y, x, c: (z, y, x + k, c) if c == 0 else (z, y + k, x, c)


def far(k):
    return lambda z, y, x, c: (z, y + k, x, c) if c == 0 else (z, y, x + k, c)


def partner(z, y, x, c):
    return (z, y, x, 1 - c)


def shifted(z, y, x, c):
    return far(2 * (z % 2))(z, y, x, c)


def shifted_partner(z, y, x, c):
    return shifted(z, y, x, 1 - c)


def params(limit):
    return pltpu.CompilerParams(vmem_limit_bytes=limit * MIB)


def project_kernel(scales, width, at_ref, v0, vp, vm, va, vb, x, xo, t, to, s_ref, so_ref, w_ref):
    piece = width and v0.shape[0] // 8
    spans = [(v0, 0, 8), (vp, 8, 8), (vm, 16, 8), (va, 24, 4), (vb, 28, 4)]
    for ref, first, count in spans:
        for k in range(count):
            row = pl.multiple_of(at_ref[first + k] * piece, piece)
            w_ref[pl.ds(row, piece), :] = ref[k * piece : (k + 1) * piece, :]
    inv_width, inv_count = scales
    column = pl.multiple_of(at_ref[32] * width, width)

    def emit(tokens, goals, out):
        proj = jnp.dot(tokens[...], w_ref[...], preferred_element_type=jnp.float32)
        scaled = (proj * inv_width - goals.astype(jnp.float32)) * inv_count
        out[...] = scaled.T.astype(jnp.bfloat16)

    emit(x, t[:, pl.ds(column, width)], s_ref)
    emit(xo, to[...], so_ref)


def term_kernel(first, count, at_ref, s, so, x, xo, out):
    side = 256

    def step(k, carry):
        column = pl.multiple_of(at_ref[first + k] * side, side)
        total = jnp.dot(s[...], x[:, pl.ds(column, side)], preferred_element_type=jnp.float32)
        total += jnp.dot(so[...], xo[:, pl.ds(column, side)], preferred_element_type=jnp.float32)
        out[:, pl.ds(pl.multiple_of(k * side, side), side)] = total.astype(out.dtype)
        return carry

    lax.fori_loop(0, count, step, 0)


def split_kernel(core_ref, own, a, b, c, mine, theirs):
    total = own[...] + a[...].astype(jnp.float32) + b[...].astype(jnp.float32) + c[...].astype(jnp.float32)
    core = core_ref[0]
    low, high = total[:, :128], total[:, 128:]
    mine[...] = jnp.where(core == 0, low, high)
    theirs[...] = jnp.where(core == 0, high, low).astype(theirs.dtype)


def inner_kernel(core_ref, rate_ref, mine, theirs, first, second, weight, new_first, new_second, pseudo):
    core = core_ref[0]
    width = mine.shape[0]
    for grads, side in ((mine, core), (theirs, 1 - core)):
        columns = pl.ds(pl.multiple_of(side * width, width), width)
        grad = grads[...].astype(jnp.float32).T
        one = 0.9 * first[:, columns] + 0.1 * grad
        two = 0.95 * second[:, columns] + 0.05 * grad * grad
        update = (one * rate_ref[1]) / (jnp.sqrt(two * rate_ref[2]) + 1e-08)
        new_first[:, columns] = one
        new_second[:, columns] = two
        pseudo[:, columns] = (rate_ref[0] * (update + 0.1 * weight[:, columns])).astype(pseudo.dtype)


def per_device(tokens, targets, kv_weight, momentum, first_moment, second_moment, step):
    f32, bf16 = jnp.float32, jnp.bfloat16
    features = tokens.shape[1]
    columns = kv_weight.shape[1]
    half = columns // 2
    width = half // NC
    z = lax.axis_index("island")
    plane = lax.axis_index("fsdp") * 4 + lax.axis_index("dp")
    core = plane % 2
    x, y = (plane // 2) % NX, plane // 8
    odd = z % 2
    scales = (1.0 / float(features) ** 0.5, 1.0 / float(tokens.shape[0] * 32) ** 0.5)

    def chip(g, m):
        outer, inner = jnp.where(core == 0, y, x) + g, jnp.where(core == 0, x, y) + m
        outer, inner = outer % 4, inner % 4
        return jnp.where(core == 0, outer * NX + inner, inner * NX + outer)

    rows_at = [
        chip(2 * odd + g, m) * 2 + (h + core) % 2 for g in (0, 1, 3, 2) for m in range(4) for h in range(2)
    ]
    rows_at = jnp.stack(rows_at + [core]).astype(jnp.int32)
    chips_at = jnp.stack([chip(g, m) for g in (2, 1, 3, 0) for m in range(4)]).astype(jnp.int32)
    core_at = core.astype(jnp.int32).reshape(1)

    whole = kv_weight.astype(bf16)
    own_half = lax.dynamic_slice_in_dim(whole, core * half, half, 1)
    other_half = lax.dynamic_slice_in_dim(whole, (1 - core) * half, half, 1)
    back = shifted
    shard = jnp.concatenate([send(own_half, back), send(other_half, shifted_partner)], axis=0)
    tokens_other = send(tokens, partner)
    goals_other = send(lax.dynamic_slice_in_dim(targets, (1 - core) * half, half, 1), partner)

    inner = [shard] + [send(shard, near(-k)) for k in (1, 2, 3)]
    block = jnp.concatenate(inner, axis=0)
    cut = block.shape[0] // 2
    vp, vm = send(block, far(-1)), send(block, far(1))
    va = send(block[:cut], lambda z, y, x, c: (z + 1, y, x, c))
    vb = send(block[cut:], lambda z, y, x, c: (z - 1, y, x, c))

    count = tokens.shape[0]
    s, so = pl.pallas_call(
        functools.partial(project_kernel, scales, width),
        out_shape=[jax.ShapeDtypeStruct((width, count), bf16)] * 2,
        in_specs=[SM] + [VM] * 9,
        out_specs=[VM] * 2,
        scratch_shapes=[pltpu.VMEM((features, width), bf16)],
        compiler_params=params(24),
        name="project",
    )(rows_at, block, vp, vm, va, vb, tokens, tokens_other, targets, goals_other)

    def terms(first, count, dtype, name):
        return pl.pallas_call(
            functools.partial(term_kernel, first, count),
            out_shape=jax.ShapeDtypeStruct((width, count * 256), dtype),
            in_specs=[SM] + [VM] * 4,
            out_specs=VM,
            compiler_params=params(24),
            name=name,
        )(chips_at, s, so, tokens, tokens_other)

    relay = terms(0, 4, bf16, "terms_relay")
    up = terms(4, 4, bf16, "terms_up")
    down = terms(8, 4, bf16, "terms_down")
    kept = terms(12, 4, f32, "terms_kept")
    mid = relay.shape[1] // 2
    from_low = send(relay[:, :mid], far(1))
    from_high = send(relay[:, mid:], far(-1))
    up_b = send(up[:, mid:], far(1))
    down_a = send(down[:, :mid], far(-1))
    up_a = send((up[:, :mid].astype(f32) + from_low.astype(f32)).astype(bf16), far(1))
    down_b = send((down[:, mid:].astype(f32) + from_high.astype(f32)).astype(bf16), far(-1))
    low = kept[:, :mid] + up_a.astype(f32) + down_a.astype(f32)
    high = kept[:, mid:] + up_b.astype(f32) + down_b.astype(f32)
    parts = [low[:, :256], low[:, 256:], high[:, :256], high[:, 256:]]
    arrived = [send(parts[k].astype(bf16), near(k)) for k in (1, 2, 3)]
    mine, theirs = pl.pallas_call(
        split_kernel,
        out_shape=[jax.ShapeDtypeStruct((width, 128), f32), jax.ShapeDtypeStruct((width, 128), bf16)],
        in_specs=[SM] + [VM] * 4,
        out_specs=[VM] * 2,
        compiler_params=params(16),
        name="split",
    )(core_at, parts[0], *arrived)
    theirs = send(theirs, partner)

    tally = step.astype(f32)
    rate = 0.1 * jnp.minimum(tally, f32(WARM)) / f32(WARM)
    rates = jnp.stack(
        [rate, 1.0 / (1.0 - jnp.power(f32(0.9), tally)), 1.0 / (1.0 - jnp.power(f32(0.95), tally))]
    )
    state = jax.ShapeDtypeStruct(kv_weight.shape, f32)
    new_first, new_second, pseudo = pl.pallas_call(
        inner_kernel,
        out_shape=[state, state, jax.ShapeDtypeStruct(kv_weight.shape, bf16)],
        in_specs=[SM] * 2 + [VM] * 5,
        out_specs=[VM] * 3,
        compiler_params=params(16),
        name="inner_step",
    )(core_at, rates, mine, theirs, first_moment[0], second_moment[0], kv_weight)

    rows = pseudo.shape[0]
    split = lax.all_to_all(pseudo.reshape(NZ, rows // NZ, columns), "island", 0, 0, tiled=True)
    share = jnp.sum(split.astype(f32), axis=0) / f32(NZ)
    spread = jnp.broadcast_to(share.astype(bf16)[None], (NZ, rows // NZ, columns))
    mean = lax.all_to_all(spread, "island", 0, 0, tiled=True).reshape(rows, columns).astype(f32)
    new_momentum = 0.9 * momentum + mean
    new_weight = kv_weight - 0.7 * (mean + 0.9 * new_momentum)
    return (new_weight, new_momentum, new_first[None], new_second[None])


def solution(mesh):
    placed = (
        P(("island", "fsdp", "dp"), None),
        P(("island", "fsdp", "dp"), None),
        P(("fsdp", "dp"), None),
        P(("fsdp", "dp"), None),
        P("island", ("fsdp", "dp"), None),
        P("island", ("fsdp", "dp"), None),
        P(),
    )
    return jax.shard_map(
        per_device,
        mesh=mesh,
        in_specs=placed,
        out_specs=(
            P(("fsdp", "dp"), None),
            P(("fsdp", "dp"), None),
            P("island", ("fsdp", "dp"), None),
            P("island", ("fsdp", "dp"), None),
        ),
        check_vma=False,
    )
```

```python
import functools
import jax
import jax.numpy as jnp
from jax import lax
from jax.experimental import pallas as pl
from jax.experimental.pallas import tpu as pltpu
from jax.sharding import PartitionSpec as P

WARM = 32
NX = NY = 4
NZ = 8
NC = 2
BIG = (768, 4096)
SIDE = 256
LIMIT_A = 10
LIMIT_B = 8
AXES = ("island", "fsdp", "dp")
MIB = 1024 * 1024
VM = pl.BlockSpec(memory_space=pltpu.VMEM)
SM = pl.BlockSpec(memory_space=pltpu.SMEM)


def flat(z, y, x, c):
    return (z % NZ) * 32 + (y % NY) * 8 + (x % NX) * 2 + c


def send(value, where):
    pairs = [
        (flat(z, y, x, c), flat(*where(z, y, x, c)))
        for z in range(NZ)
        for y in range(NY)
        for x in range(NX)
        for c in range(2)
    ]
    return lax.ppermute(value, AXES, pairs)


def near(k):
    return lambda z, y, x, c: (z, y, x + k, c) if c == 0 else (z, y + k, x, c)


def far(k):
    return lambda z, y, x, c: (z, y + k, x, c) if c == 0 else (z, y, x + k, c)


def partner(z, y, x, c):
    return (z, y, x, 1 - c)


def params(limit):
    return pltpu.CompilerParams(vmem_limit_bytes=limit * MIB)


def here():
    fsdp, dp = lax.axis_index("fsdp"), lax.axis_index("dp")
    return lax.div(fsdp, 2), lax.rem(fsdp, 2) * 2 + lax.div(dp, 2), lax.rem(dp, 2)


def chip(place, g, m):
    y, x, core = place
    outer = lax.rem(jnp.where(core == 0, y, x) + g, 4)
    inner = lax.rem(jnp.where(core == 0, x, y) + m, 4)
    return jnp.where(core == 0, outer * NX + inner, inner * NX + outer)


def term(place, g, m, s, so, x, xo):
    columns = pl.ds(pl.multiple_of(chip(place, g, m) * SIDE, SIDE), SIDE)
    total = jnp.dot(s[...], x[:, columns], preferred_element_type=jnp.float32)
    return total + jnp.dot(so[...], xo[:, columns], preferred_element_type=jnp.float32)


def project_kernel(scales, j, v0, v1, v3, v2, x, xo, t, to, s_ref, so_ref, relay, w_ref):
    place = here()
    core = place[2]
    width = v0.shape[1]
    piece = SIDE // 2
    for g, ref in ((0, v0), (1, v1), (3, v3), (2, v2)):
        for m in range(4):
            for h in range(2):
                row = chip(place, g, m) * SIDE + lax.rem(core + h, 2) * piece
                first = m * SIDE + h * piece
                w_ref[pl.ds(pl.multiple_of(row, piece), piece), :] = ref[first : first + piece, :]
    inv_width, inv_count = scales
    column = pl.multiple_of((core * NC + j) * width, width)

    def emit(tokens, goals, out):
        proj = jnp.dot(tokens[...], w_ref[...], preferred_element_type=jnp.float32)
        scaled = (proj * inv_width - goals.astype(jnp.float32)) * inv_count
        out[...] = scaled.T.astype(jnp.bfloat16)

    emit(xo, to[:, j * width : (j + 1) * width], so_ref)
    emit(x, t[:, pl.ds(column, width)], s_ref)
    for m in range(4):
        relay[:, m * SIDE : (m + 1) * SIDE] = term(place, 2, m, s_ref, so_ref, x, xo).astype(relay.dtype)


def sides_kernel(s, so, x, xo, up, down):
    place = here()
    for g, out in ((1, up), (3, down)):
        for m in range(4):
            out[:, m * SIDE : (m + 1) * SIDE] = term(place, g, m, s, so, x, xo).astype(out.dtype)


def kept_kernel(*refs):
    x, xo, out = refs[-3:]
    place = here()
    for j in range(NC):
        s, so = refs[2 * j : 2 * j + 2]
        width = s.shape[0]
        for m in range(4):
            out[j * width : (j + 1) * width, m * SIDE : (m + 1) * SIDE] = term(place, 0, m, s, so, x, xo)


def fold_kernel(*refs):
    kept, arrived, outs = refs[0], refs[1 : 1 + 3 * NC], refs[1 + 3 * NC :]
    width = arrived[0].shape[0]
    for j in range(NC):
        rows = slice(j * width, (j + 1) * width)
        for m in range(4):
            columns = slice(m * SIDE, (m + 1) * SIDE)
            total = kept[rows, columns]
            for ref in arrived[3 * j : 3 * j + 3]:
                total += ref[:, columns].astype(jnp.float32)
            outs[m][rows, :] = total.astype(outs[m].dtype)


def split_kernel(own, a, b, c, mine, theirs):
    total = own[...] + a[...].astype(jnp.float32) + b[...].astype(jnp.float32) + c[...].astype(jnp.float32)
    core = here()[2]
    low, high = total[:, : SIDE // 2], total[:, SIDE // 2 :]
    mine[...] = jnp.where(core == 0, low, high)
    theirs[...] = jnp.where(core == 0, high, low).astype(theirs.dtype)


def inner_kernel(rate_ref, mine, theirs, first, second, weight, new_first, new_second, pseudo):
    core = here()[2]
    width = mine.shape[0]
    for grads, side in ((mine, core), (theirs, 1 - core)):
        columns = pl.ds(pl.multiple_of(side * width, width), width)
        grad = grads[...].astype(jnp.float32).T
        one = 0.9 * first[:, columns] + 0.1 * grad
        two = 0.95 * second[:, columns] + 0.05 * grad * grad
        update = (one * rate_ref[1]) / (jnp.sqrt(two * rate_ref[2]) + 1e-08)
        new_first[:, columns] = one
        new_second[:, columns] = two
        pseudo[:, columns] = (rate_ref[0] * (update + 0.1 * weight[:, columns])).astype(pseudo.dtype)


def local(kernel, shapes, limit, name, *operands, scratch=(), scalars=0):
    operands = [
        pltpu.with_memory_space_constraint(o, pltpu.VMEM) if o.shape == BIG else o for o in operands
    ]
    return pl.pallas_call(
        kernel,
        out_shape=[jax.ShapeDtypeStruct(*s) for s in shapes],
        in_specs=[SM] * scalars + [VM] * (len(operands) - scalars),
        out_specs=[VM] * len(shapes),
        scratch_shapes=list(scratch),
        compiler_params=params(limit),
        name=name,
    )(*operands)


def per_device(tokens, targets, kv_weight, momentum, first_moment, second_moment, step):
    f32, bf16 = jnp.float32, jnp.bfloat16
    count, features = tokens.shape
    rows, columns = kv_weight.shape
    half = columns // 2
    width = half // NC
    core = here()[2]
    scales = (1.0 / float(features) ** 0.5, 1.0 / float(count * 32) ** 0.5)

    whole = kv_weight.astype(bf16)
    own_half = lax.dynamic_slice_in_dim(whole, core * half, half, 1)
    other_half = lax.dynamic_slice_in_dim(whole, (1 - core) * half, half, 1)
    crossed = send(other_half, partner)
    crossed, tokens_now = lax.optimization_barrier((crossed, tokens))
    tokens_other = send(tokens_now, partner)
    shard = jnp.concatenate([own_half, crossed], axis=0)
    goals_other = send(lax.dynamic_slice_in_dim(targets, (1 - core) * half, half, 1), partner)

    inner = [shard] + [send(shard, near(-k)) for k in (1, 2, 3)]
    scaled, arrived = [], []
    for j in range(NC):
        block = jnp.concatenate([p[:, j * width : (j + 1) * width] for p in inner], axis=0)
        if j > 0:
            block, v1, v3, v2 = lax.optimization_barrier((block, v1, v3, v2))
        v1, v3, v2 = send(block, far(-1)), send(block, far(1)), send(block, far(2))
        s, so, relay = local(
            functools.partial(project_kernel, scales, j),
            [((width, count), bf16)] * 2 + [((width, 4 * SIDE), bf16)],
            LIMIT_A,
            "project",
            block, v1, v3, v2, tokens, tokens_other, targets, goals_other,
            scratch=[pltpu.VMEM((features, width), bf16)],
        )
        up, down = local(
            sides_kernel, [((width, 4 * SIDE), bf16)] * 2, LIMIT_B, "sides", s, so, tokens, tokens_other
        )
        scaled += [s, so]
        arrived += [send(relay, far(2)), send(up, far(1)), send(down, far(-1))]

    (kept,) = local(
        kept_kernel, [((half, 4 * SIDE), f32)], LIMIT_B, "kept", *scaled, tokens, tokens_other
    )
    parts = local(
        fold_kernel, [((half, SIDE), f32)] + [((half, SIDE), bf16)] * 3, LIMIT_B, "fold", kept, *arrived
    )
    mine, theirs = local(
        split_kernel,
        [((half, SIDE // 2), f32), ((half, SIDE // 2), bf16)],
        LIMIT_B,
        "split",
        parts[0], *[send(parts[k], near(k)) for k in (1, 2, 3)],
    )
    theirs = send(theirs, partner)

    tally = step.astype(f32)
    rate = 0.1 * jnp.minimum(tally, f32(WARM)) / f32(WARM)
    rates = jnp.stack(
        [rate, 1.0 / (1.0 - jnp.power(f32(0.9), tally)), 1.0 / (1.0 - jnp.power(f32(0.95), tally))]
    )
    state = (kv_weight.shape, f32)
    new_first, new_second, pseudo = local(
        inner_kernel,
        [state, state, (kv_weight.shape, bf16)],
        LIMIT_B,
        "inner_step",
        rates, mine, theirs, first_moment[0], second_moment[0], kv_weight,
        scalars=1,
    )

    split = lax.all_to_all(pseudo.reshape(NZ, rows // NZ, columns), "island", 0, 0, tiled=True)
    share = jnp.sum(split.astype(f32), axis=0) / f32(NZ)
    spread = jnp.broadcast_to(share.astype(bf16)[None], (NZ, rows // NZ, columns))
    mean = lax.all_to_all(spread, "island", 0, 0, tiled=True).reshape(rows, columns).astype(f32)
    new_momentum = 0.9 * momentum + mean
    new_weight = kv_weight - 0.7 * (mean + 0.9 * new_momentum)
    return (new_weight, new_momentum, new_first[None], new_second[None])


def solution(mesh):
    placed = (
        P(("island", "fsdp", "dp"), None),
        P(("island", "fsdp", "dp"), None),
        P(("fsdp", "dp"), None),
        P(("fsdp", "dp"), None),
        P("island", ("fsdp", "dp"), None),
        P("island", ("fsdp", "dp"), None),
        P(),
    )
    return jax.shard_map(
        per_device,
        mesh=mesh,
        in_specs=placed,
        out_specs=(
            P(("fsdp", "dp"), None),
            P(("fsdp", "dp"), None),
            P("island", ("fsdp", "dp"), None),
            P("island", ("fsdp", "dp"), None),
        ),
        check_vma=False,
    )
```

```python
import functools
import jax
import jax.numpy as jnp
from jax import lax
from jax.experimental import pallas as pl
from jax.experimental.pallas import tpu as pltpu
from jax.sharding import PartitionSpec as P

WARM = 32
NX = NY = 4
NZ = 8
BIG = (768, 4096)
SIDE = 256
STEPS = 3
LOW, HIGH = (0, 1), (2, 3)
LIMIT_A = 10
LIMIT_B = 8
AXES = ("island", "fsdp", "dp")
MIB = 1024 * 1024
GIGA = 10**9
VM = pl.BlockSpec(memory_space=pltpu.VMEM)
SM = pl.BlockSpec(memory_space=pltpu.SMEM)


def flat(z, y, x, c):
    return (z % NZ) * 32 + (y % NY) * 8 + (x % NX) * 2 + c


def send(value, where):
    pairs = [
        (flat(z, y, x, c), flat(*where(z, y, x, c)))
        for z in range(NZ)
        for y in range(NY)
        for x in range(NX)
        for c in range(2)
    ]
    return lax.ppermute(value, AXES, pairs)


def near(k):
    return lambda z, y, x, c: (z, y, x + k, c) if c == 0 else (z, y + k, x, c)


def far(k):
    return lambda z, y, x, c: (z, y + k, x, c) if c == 0 else (z, y, x + k, c)


def partner(z, y, x, c):
    return (z, y, x, 1 - c)


def params(limit):
    return pltpu.CompilerParams(vmem_limit_bytes=limit * MIB)


def here():
    fsdp, dp = lax.axis_index("fsdp"), lax.axis_index("dp")
    return lax.div(fsdp, 2), lax.rem(fsdp, 2) * 2 + lax.div(dp, 2), lax.rem(dp, 2)


def chip(place, g, m):
    y, x, core = place
    outer = lax.rem(jnp.where(core == 0, y, x) + g, 4)
    inner = lax.rem(jnp.where(core == 0, x, y) + m, 4)
    return jnp.where(core == 0, outer * NX + inner, inner * NX + outer)


def columns_of(place, g, m):
    return pl.ds(pl.multiple_of(chip(place, g, m) * SIDE, SIDE), SIDE)


def term(place, g, m, s, so, x, xo):
    columns = columns_of(place, g, m)
    total = jnp.dot(s[...], x[:, columns], preferred_element_type=jnp.float32)
    return total + jnp.dot(so[...], xo[:, columns], preferred_element_type=jnp.float32)


def product(place, tokens, g, members, block, span=slice(None)):
    rows = [tokens[span, columns_of(place, g, m)] for m in members]
    return jnp.dot(jnp.concatenate(rows, axis=1), block, preferred_element_type=jnp.float32)


def first_kernel(a, b, c, d, x, xo, out, out_other, held, held_other, sems):
    place = here()
    rows = x.shape[0] // STEPS
    copies = []
    for i, (source, into) in enumerate(((x, held), (xo, held_other))):
        for k in range(STEPS):
            span = pl.ds(k * rows, rows)
            copies.append(pltpu.make_async_copy(source.at[span], into.at[span], sems.at[i, k]))
    for copy in copies:
        copy.start()
    block = jnp.concatenate([a[...], b[...], c[...], d[...]], axis=0)
    for i, (tokens, ref) in enumerate(((held, out), (held_other, out_other))):
        for k in range(STEPS):
            copies[i * STEPS + k].wait()
            span = slice(k * rows, (k + 1) * rows)
            ref[span, :] = product(place, tokens, 0, range(4), block, span).astype(ref.dtype)


def more_kernel(acc, acc_other, low_1, high_1, low_3, high_3, x, xo, out, out_other):
    place = here()
    blocks = ((1, (low_1, high_1)), (3, (low_3, high_3)))
    blocks = [(g, jnp.concatenate([ref[...] for ref in refs], axis=0)) for g, refs in blocks]
    for tokens, start, ref in ((x, acc, out), (xo, acc_other, out_other)):
        total = start[...].astype(jnp.float32)
        for g, block in blocks:
            total += product(place, tokens, g, range(4), block)
        ref[...] = total.astype(ref.dtype)


def late_kernel(scales, acc, acc_other, va, vb, x, xo, rates, t, to, s_ref, so_ref, relay_a, relay_b, rates_out, aims, sems):
    place = here()
    copies = [pltpu.make_async_copy(ref, aims.at[i], sems.at[i]) for i, ref in enumerate((t, to))]
    for copy in copies:
        copy.start()
    inv_width, inv_count = scales
    rates_out[...] = rates[...]
    for i, (tokens, total, out) in enumerate(((x, acc, s_ref), (xo, acc_other, so_ref))):
        proj = total[...].astype(jnp.float32) + product(place, tokens, 2, LOW, va[...]) + product(place, tokens, 2, HIGH, vb[...])
        copies[i].wait()
        scaled = (proj * inv_width - aims[i].astype(jnp.float32)) * inv_count
        out[...] = scaled.T.astype(jnp.bfloat16)
    for out, members in ((relay_a, LOW), (relay_b, HIGH)):
        for k, m in enumerate(members):
            out[:, k * SIDE : (k + 1) * SIDE] = term(place, 2, m, s_ref, so_ref, x, xo).astype(out.dtype)


def sides_kernel(members, s, so, x, xo, up, down):
    place = here()
    for g, out, chosen in ((1, up, members[0]), (3, down, members[1])):
        for k, m in enumerate(chosen):
            out[:, k * SIDE : (k + 1) * SIDE] = term(place, g, m, s, so, x, xo).astype(out.dtype)


def kept_kernel(s, so, x, xo, out):
    place = here()
    for m in range(4):
        out[:, m * SIDE : (m + 1) * SIDE] = term(place, 0, m, s, so, x, xo)


def fold_kernel(kept, up_a, down_a, up_b, down_b, *outs):
    for m in range(4):
        part = slice(m % 2 * SIDE, (m % 2 + 1) * SIDE)
        total = kept[:, m * SIDE : (m + 1) * SIDE]
        for ref in (up_a, down_a) if m < 2 else (up_b, down_b):
            total += ref[:, part].astype(jnp.float32)
        outs[m][...] = total.astype(outs[m].dtype)


def split_kernel(own, a, b, c, mine, theirs):
    total = own[...] + a[...].astype(jnp.float32) + b[...].astype(jnp.float32) + c[...].astype(jnp.float32)
    core = here()[2]
    low, high = total[:, : SIDE // 2], total[:, SIDE // 2 :]
    mine[...] = jnp.where(core == 0, low, high)
    theirs[...] = jnp.where(core == 0, high, low).astype(theirs.dtype)


def inner_kernel(rates, first, second, weight, *refs):
    grads, (new_first, new_second, pseudo) = refs[:-3], refs[-3:]
    core = here()[2]
    width = grads[0].shape[0]
    rate, first_scale, second_scale = rates[0:1, :], rates[1:2, :], rates[2:3, :]
    for k, ref in enumerate(grads):
        side = core if k % 2 == 0 else 1 - core
        columns = pl.ds(pl.multiple_of(side * width, width), width)
        grad = ref[...].astype(jnp.float32).T
        one = 0.9 * first[:, columns] + 0.1 * grad
        two = 0.95 * second[:, columns] + 0.05 * grad * grad
        update = (one * first_scale) / (jnp.sqrt(two * second_scale) + 1e-08)
        new_first[:, columns] = one
        new_second[:, columns] = two
        pseudo[:, columns] = (rate * (update + 0.1 * weight[:, columns])).astype(pseudo.dtype)


def local(kernel, shapes, limit, name, *operands, cost=1, alias={}):
    operands = [
        pltpu.with_memory_space_constraint(o, pltpu.VMEM) if o.shape == BIG else o for o in operands
    ]
    return pl.pallas_call(
        kernel,
        out_shape=[jax.ShapeDtypeStruct(*s) for s in shapes],
        in_specs=[VM] * len(operands),
        out_specs=[VM] * len(shapes),
        compiler_params=params(limit),
        input_output_aliases=alias,
        cost_estimate=pl.CostEstimate(flops=cost * GIGA, bytes_accessed=MIB, transcendentals=0),
        name=name,
    )(*operands)


def per_device(tokens, targets, kv_weight, momentum, first_moment, second_moment, step):
    f32, bf16 = jnp.float32, jnp.bfloat16
    count, features = tokens.shape
    rows, columns = kv_weight.shape
    half = columns // 2
    core = here()[2]
    scales = (1.0 / float(features) ** 0.5, 1.0 / float(count * 32) ** 0.5)

    whole = kv_weight.astype(bf16)
    own_half = lax.dynamic_slice_in_dim(whole, core * half, half, 1)
    other_half = lax.dynamic_slice_in_dim(whole, (1 - core) * half, half, 1)
    crossed = send(other_half, partner)
    crossed, tokens_now = lax.optimization_barrier((crossed, tokens))
    tokens_other = send(tokens_now, partner)
    shard = jnp.where(
        core == 0,
        jnp.concatenate([own_half, crossed], axis=0),
        jnp.concatenate([crossed, own_half], axis=0),
    )
    inner = [shard] + [send(shard, near(-k)) for k in (1, 2, 3)]
    tally = step.astype(f32)
    rate = 0.1 * jnp.minimum(tally, f32(WARM)) / f32(WARM)
    first_scale = 1.0 / (1.0 - jnp.power(f32(0.9), tally))
    second_scale = 1.0 / (1.0 - jnp.power(f32(0.95), tally))
    rates = jnp.stack([rate, first_scale, second_scale] + [rate] * 5)
    rates = jnp.broadcast_to(rates[:, None], (8, half))

    inner[3], targets = lax.optimization_barrier((inner[3], targets))
    goals = lax.dynamic_slice_in_dim(targets, core * half, half, 1)
    goals_other = lax.dynamic_slice_in_dim(targets, (1 - core) * half, half, 1)
    inner[2], goals, goals_other = lax.optimization_barrier((inner[2], goals, goals_other))
    goals_other = send(goals_other, partner)
    low, high = jnp.concatenate(inner[:2], axis=0), jnp.concatenate(inner[2:], axis=0)
    low, tokens_other = lax.optimization_barrier((low, tokens_other))
    low_1, high_3 = send(low, far(-1)), send(high, far(1))
    high_1, low_3 = send(high, far(-1)), send(low, far(1))
    low_2, high_2 = send(low_1, far(-1)), send(high_3, far(1))
    hbm = pl.BlockSpec(memory_space=pltpu.HBM)
    *acc, tokens, tokens_other = pl.pallas_call(
        first_kernel,
        out_shape=[jax.ShapeDtypeStruct((count, half), bf16)] * 2 + [pltpu.VMEM(tokens.shape, bf16)] * 2,
        in_specs=[VM] * 4 + [hbm] * 2,
        out_specs=[VM] * 4,
        scratch_shapes=[pltpu.SemaphoreType.DMA((2, STEPS))],
        compiler_params=params(LIMIT_A),
        name="first",
    )(
        *inner,
        pltpu.with_memory_space_constraint(tokens, pltpu.HBM),
        pltpu.with_memory_space_constraint(tokens_other, pltpu.HBM),
    )
    pair = (tokens, tokens_other)
    acc = local(
        more_kernel, [((count, half), bf16)] * 2, LIMIT_A, "more", *acc, low_1, high_1, low_3, high_3, *pair, cost=4
    )
    mid = ((half, 2 * SIDE), bf16)
    s, so, relay_a, relay_b, rates = pl.pallas_call(
        functools.partial(late_kernel, scales),
        out_shape=[
            jax.ShapeDtypeStruct(*k) for k in [((half, count), bf16)] * 2 + [mid] * 2 + [(rates.shape, f32)]
        ],
        in_specs=[VM] * 7 + [pl.BlockSpec(memory_space=pltpu.HBM)] * 2,
        out_specs=[VM] * 5,
        scratch_shapes=[pltpu.VMEM((2, count, half), bf16), pltpu.SemaphoreType.DMA((2,))],
        compiler_params=params(LIMIT_A),
        name="late",
    )(
        *acc,
        low_2, high_2,
        *[pltpu.with_memory_space_constraint(k, pltpu.VMEM) for k in pair],
        rates,
        *[pltpu.with_memory_space_constraint(k, pltpu.HBM) for k in (goals, goals_other)],
    )
    sides = functools.partial(sides_kernel, (HIGH, LOW))
    up_b, down_a = local(sides, [mid] * 2, LIMIT_B, "sides_near", s, so, *pair, cost=2)
    sides = functools.partial(sides_kernel, (LOW, HIGH))
    up_a, down_b = local(sides, [mid] * 2, LIMIT_B, "sides_rest", s, so, *pair, cost=2)
    (kept,) = local(kept_kernel, [((half, 4 * SIDE), f32)], LIMIT_B, "kept", s, so, *pair, cost=2)
    from_low, from_high = send(relay_a, far(1)), send(relay_b, far(-1))
    up_b, down_a = send(up_b, far(1)), send(down_a, far(-1))
    up_a = send((up_a.astype(f32) + from_low.astype(f32)).astype(bf16), far(1))
    down_b = send((down_b.astype(f32) + from_high.astype(f32)).astype(bf16), far(-1))
    parts = local(
        fold_kernel,
        [((half, SIDE), f32)] + [((half, SIDE), bf16)] * 3,
        LIMIT_B,
        "fold",
        kept, up_a, down_a, up_b, down_b,
    )
    mine, theirs = local(
        split_kernel,
        [((half, SIDE // 2), f32), ((half, SIDE // 2), bf16)],
        LIMIT_B,
        "split",
        parts[0], *[send(parts[k], near(k)) for k in (1, 2, 3)],
    )
    grads = [mine, send(theirs, partner)]

    state = (kv_weight.shape, f32)
    new_first, new_second, pseudo = local(
        inner_kernel,
        [state, state, (kv_weight.shape, bf16)],
        LIMIT_B,
        "inner_step",
        rates, first_moment[0], second_moment[0], kv_weight, *grads,
    )

    split = lax.all_to_all(pseudo.reshape(NZ, rows // NZ, columns), "island", 0, 0, tiled=True)
    share = jnp.sum(split.astype(f32), axis=0) / f32(NZ)
    spread = jnp.broadcast_to(share.astype(bf16)[None], (NZ, rows // NZ, columns))
    mean = lax.all_to_all(spread, "island", 0, 0, tiled=True).reshape(rows, columns).astype(f32)
    new_momentum = 0.9 * momentum + mean
    new_weight = kv_weight - 0.7 * (mean + 0.9 * new_momentum)
    return (new_weight, new_momentum, new_first[None], new_second[None])


def solution(mesh):
    placed = (
        P(("island", "fsdp", "dp"), None),
        P(("island", "fsdp", "dp"), None),
        P(("fsdp", "dp"), None),
        P(("fsdp", "dp"), None),
        P("island", ("fsdp", "dp"), None),
        P("island", ("fsdp", "dp"), None),
        P(),
    )
    return jax.shard_map(
        per_device,
        mesh=mesh,
        in_specs=placed,
        out_specs=(
            P(("fsdp", "dp"), None),
            P(("fsdp", "dp"), None),
            P("island", ("fsdp", "dp"), None),
            P("island", ("fsdp", "dp"), None),
        ),
        check_vma=False,
    )
```

```python
import functools
import jax
import jax.numpy as jnp
from jax import lax
from jax.experimental import pallas as pl
from jax.experimental.pallas import tpu as pltpu
from jax.sharding import PartitionSpec as P

WARM = 32
NX = NY = 4
NZ = 8
BIG = (768, 4096)
SIDE = 256
STEPS = 3
LOW, HIGH = (0, 1), (2, 3)
LIMIT_A = 10
LIMIT_B = 8
AXES = ("island", "fsdp", "dp")
MIB = 1024 * 1024
GIGA = 10**9
VM = pl.BlockSpec(memory_space=pltpu.VMEM)
SM = pl.BlockSpec(memory_space=pltpu.SMEM)


def flat(z, y, x, c):
    return (z % NZ) * 32 + (y % NY) * 8 + (x % NX) * 2 + c


def send(value, where):
    pairs = [
        (flat(z, y, x, c), flat(*where(z, y, x, c)))
        for z in range(NZ)
        for y in range(NY)
        for x in range(NX)
        for c in range(2)
    ]
    return lax.ppermute(value, AXES, pairs)


def near(k):
    return lambda z, y, x, c: (z, y, x + k, c) if c == 0 else (z, y + k, x, c)


def far(k):
    return lambda z, y, x, c: (z, y + k, x, c) if c == 0 else (z, y, x + k, c)


def partner(z, y, x, c):
    return (z, y, x, 1 - c)


def params(limit):
    return pltpu.CompilerParams(vmem_limit_bytes=limit * MIB)


def here():
    fsdp, dp = lax.axis_index("fsdp"), lax.axis_index("dp")
    return lax.div(fsdp, 2), lax.rem(fsdp, 2) * 2 + lax.div(dp, 2), lax.rem(dp, 2)


def chip(place, g, m):
    y, x, core = place
    outer = lax.rem(jnp.where(core == 0, y, x) + g, 4)
    inner = lax.rem(jnp.where(core == 0, x, y) + m, 4)
    return jnp.where(core == 0, outer * NX + inner, inner * NX + outer)


def columns_of(place, g, m):
    return pl.ds(pl.multiple_of(chip(place, g, m) * SIDE, SIDE), SIDE)


def term(place, g, m, s, so, x, xo):
    columns = columns_of(place, g, m)
    total = jnp.dot(s[...], x[:, columns], preferred_element_type=jnp.float32)
    return total + jnp.dot(so[...], xo[:, columns], preferred_element_type=jnp.float32)


def product(place, tokens, g, members, block, span=slice(None)):
    rows = [tokens[span, columns_of(place, g, m)] for m in members]
    return jnp.dot(jnp.concatenate(rows, axis=1), block, preferred_element_type=jnp.float32)


def first_kernel(a, b, c, d, x, xo, out, out_other, held, held_other, sems):
    place = here()
    rows = x.shape[0] // STEPS
    copies = []
    for i, (source, into) in enumerate(((x, held), (xo, held_other))):
        for k in range(STEPS):
            span = pl.ds(k * rows, rows)
            copies.append(pltpu.make_async_copy(source.at[span], into.at[span], sems.at[i, k]))
    for copy in copies:
        copy.start()
    block = jnp.concatenate([a[...], b[...], c[...], d[...]], axis=0)
    for i, (tokens, ref) in enumerate(((held, out), (held_other, out_other))):
        for k in range(STEPS):
            copies[i * STEPS + k].wait()
            span = slice(k * rows, (k + 1) * rows)
            ref[span, :] = product(place, tokens, 0, range(4), block, span).astype(ref.dtype)


def more_kernel(acc, acc_other, low_1, high_1, low_3, high_3, x, xo, out, out_other):
    place = here()
    blocks = ((1, (low_1, high_1)), (3, (low_3, high_3)))
    blocks = [(g, jnp.concatenate([ref[...] for ref in refs], axis=0)) for g, refs in blocks]
    for tokens, start, ref in ((x, acc, out), (xo, acc_other, out_other)):
        total = start[...].astype(jnp.float32)
        for g, block in blocks:
            total += product(place, tokens, g, range(4), block)
        ref[...] = total.astype(ref.dtype)


def stack_kernel(a, b, out):
    rows = a.shape[0]
    out[:rows, :] = a[...]
    out[rows:, :] = b[...]


def late_kernel(scales, acc, acc_other, va, vb, x, xo, to, t, s_ref, so_ref, relay_a, relay_b, aims, sem):
    place = here()
    fetch = pltpu.make_async_copy(t, aims, sem)
    fetch.start()
    inv_width, inv_count = scales
    for tokens, total, goals, out in ((xo, acc_other, to, so_ref), (x, acc, aims, s_ref)):
        proj = total[...].astype(jnp.float32) + product(place, tokens, 2, LOW, va[...]) + product(place, tokens, 2, HIGH, vb[...])
        if goals is aims:
            fetch.wait()
        scaled = (proj * inv_width - goals[...].astype(jnp.float32)) * inv_count
        out[...] = scaled.T.astype(jnp.bfloat16)
    for out, members in ((relay_a, LOW), (relay_b, HIGH)):
        for k, m in enumerate(members):
            out[:, k * SIDE : (k + 1) * SIDE] = term(place, 2, m, s_ref, so_ref, x, xo).astype(out.dtype)


def sides_kernel(members, s, so, x, xo, up, down):
    place = here()
    for g, out, chosen in ((1, up, members[0]), (3, down, members[1])):
        for k, m in enumerate(chosen):
            out[:, k * SIDE : (k + 1) * SIDE] = term(place, g, m, s, so, x, xo).astype(out.dtype)


def kept_kernel(s, so, x, xo, out):
    place = here()
    for m in range(4):
        out[:, m * SIDE : (m + 1) * SIDE] = term(place, 0, m, s, so, x, xo)


def fold_kernel(kept, up_a, down_a, up_b, down_b, *outs):
    for m in range(4):
        part = slice(m % 2 * SIDE, (m % 2 + 1) * SIDE)
        total = kept[:, m * SIDE : (m + 1) * SIDE]
        for ref in (up_a, down_a) if m < 2 else (up_b, down_b):
            total += ref[:, part].astype(jnp.float32)
        outs[m][...] = total.astype(outs[m].dtype)


def split_kernel(own, a, b, c, rates, mine, theirs, rates_out):
    rates_out[...] = rates[...]
    total = own[...] + a[...].astype(jnp.float32) + b[...].astype(jnp.float32) + c[...].astype(jnp.float32)
    core = here()[2]
    low, high = total[:, : SIDE // 2], total[:, SIDE // 2 :]
    mine[...] = jnp.where(core == 0, low, high)
    theirs[...] = jnp.where(core == 0, high, low).astype(theirs.dtype)


def inner_kernel(rates, first, second, weight, *refs):
    grads, (new_first, new_second, pseudo) = refs[:-3], refs[-3:]
    core = here()[2]
    width = grads[0].shape[0]
    rate, first_scale, second_scale = rates[0:1, :], rates[1:2, :], rates[2:3, :]
    for k, ref in enumerate(grads):
        side = core if k % 2 == 0 else 1 - core
        columns = pl.ds(pl.multiple_of(side * width, width), width)
        grad = ref[...].astype(jnp.float32).T
        one = 0.9 * first[:, columns] + 0.1 * grad
        two = 0.95 * second[:, columns] + 0.05 * grad * grad
        update = (one * first_scale) / (jnp.sqrt(two * second_scale) + 1e-08)
        new_first[:, columns] = one
        new_second[:, columns] = two
        pseudo[:, columns] = (rate * (update + 0.1 * weight[:, columns])).astype(pseudo.dtype)


def local(kernel, shapes, limit, name, *operands, cost=1, alias={}):
    operands = [
        pltpu.with_memory_space_constraint(o, pltpu.VMEM) if o.shape == BIG else o for o in operands
    ]
    return pl.pallas_call(
        kernel,
        out_shape=[jax.ShapeDtypeStruct(*s) for s in shapes],
        in_specs=[VM] * len(operands),
        out_specs=[VM] * len(shapes),
        compiler_params=params(limit),
        input_output_aliases=alias,
        cost_estimate=pl.CostEstimate(flops=cost * GIGA, bytes_accessed=MIB, transcendentals=0),
        name=name,
    )(*operands)


def per_device(tokens, targets, kv_weight, momentum, first_moment, second_moment, step):
    f32, bf16 = jnp.float32, jnp.bfloat16
    count, features = tokens.shape
    rows, columns = kv_weight.shape
    half = columns // 2
    core = here()[2]
    scales = (1.0 / float(features) ** 0.5, 1.0 / float(count * 32) ** 0.5)

    whole = kv_weight.astype(bf16)
    own_half = lax.dynamic_slice_in_dim(whole, core * half, half, 1)
    other_half = lax.dynamic_slice_in_dim(whole, (1 - core) * half, half, 1)
    crossed = send(other_half, partner)
    crossed, tokens_now = lax.optimization_barrier((crossed, tokens))
    tokens_other = send(tokens_now, partner)
    shard = jnp.where(
        core == 0,
        jnp.concatenate([own_half, crossed], axis=0),
        jnp.concatenate([crossed, own_half], axis=0),
    )
    inner = [shard] + [send(shard, near(-k)) for k in (1, 2, 3)]
    tally = step.astype(f32)
    rate = 0.1 * jnp.minimum(tally, f32(WARM)) / f32(WARM)
    first_scale = 1.0 / (1.0 - jnp.power(f32(0.9), tally))
    second_scale = 1.0 / (1.0 - jnp.power(f32(0.95), tally))
    rates = jnp.stack([rate, first_scale, second_scale] + [rate] * 5)
    rates = jnp.broadcast_to(rates[:, None], (8, half))

    inner[3], targets = lax.optimization_barrier((inner[3], targets))
    goals = lax.dynamic_slice_in_dim(targets, core * half, half, 1)
    goals_other = lax.dynamic_slice_in_dim(targets, (1 - core) * half, half, 1)
    inner[2], goals, goals_other = lax.optimization_barrier((inner[2], goals, goals_other))
    goals_other = send(goals_other, partner)
    both = [((2 * inner[0].shape[0], half), bf16)]
    (high,) = local(stack_kernel, both, LIMIT_B, "stack", *inner[2:])
    (low,) = local(stack_kernel, both, LIMIT_B, "stack", *inner[:2])
    low, tokens_other = lax.optimization_barrier((low, tokens_other))
    low_1, high_3 = send(low, far(-1)), send(high, far(1))
    low_3 = send(low, far(1))
    high_1 = send(high, far(-1))
    low_2, high_2 = send(low_1, far(-1)), send(high_3, far(1))
    hbm = pl.BlockSpec(memory_space=pltpu.HBM)
    *acc, tokens, tokens_other = pl.pallas_call(
        first_kernel,
        out_shape=[jax.ShapeDtypeStruct((count, half), bf16)] * 2 + [pltpu.VMEM(tokens.shape, bf16)] * 2,
        in_specs=[VM] * 4 + [hbm] * 2,
        out_specs=[VM] * 4,
        scratch_shapes=[pltpu.SemaphoreType.DMA((2, STEPS))],
        compiler_params=params(LIMIT_A),
        name="first",
    )(
        *inner,
        pltpu.with_memory_space_constraint(tokens, pltpu.HBM),
        pltpu.with_memory_space_constraint(tokens_other, pltpu.HBM),
    )
    pair = (tokens, tokens_other)
    acc = local(
        more_kernel, [((count, half), bf16)] * 2, LIMIT_A, "more", *acc, low_1, high_1, low_3, high_3, *pair, cost=4
    )
    mid = ((half, 2 * SIDE), bf16)
    s, so, relay_a, relay_b = pl.pallas_call(
        functools.partial(late_kernel, scales),
        out_shape=[
            jax.ShapeDtypeStruct(*k) for k in [((half, count), bf16)] * 2 + [mid] * 2
        ],
        in_specs=[VM] * 7 + [hbm],
        out_specs=[VM] * 4,
        scratch_shapes=[pltpu.VMEM((count, half), bf16), pltpu.SemaphoreType.DMA],
        compiler_params=params(LIMIT_A),
        name="late",
    )(
        *acc,
        low_2, high_2,
        *[pltpu.with_memory_space_constraint(k, pltpu.VMEM) for k in pair],
        goals_other,
        pltpu.with_memory_space_constraint(goals, pltpu.HBM),
    )
    sides = functools.partial(sides_kernel, (HIGH, LOW))
    up_b, down_a = local(sides, [mid] * 2, LIMIT_B, "sides_near", s, so, *pair, cost=2)
    sides = functools.partial(sides_kernel, (LOW, HIGH))
    up_a, down_b = local(sides, [mid] * 2, LIMIT_B, "sides_rest", s, so, *pair, cost=2)
    (kept,) = local(kept_kernel, [((half, 4 * SIDE), f32)], LIMIT_B, "kept", s, so, *pair, cost=2)
    from_low, from_high = send(relay_a, far(1)), send(relay_b, far(-1))
    up_b, down_a = send(up_b, far(1)), send(down_a, far(-1))
    up_a = send((up_a.astype(f32) + from_low.astype(f32)).astype(bf16), far(1))
    down_b = send((down_b.astype(f32) + from_high.astype(f32)).astype(bf16), far(-1))
    parts = local(
        fold_kernel,
        [((half, SIDE), f32)] + [((half, SIDE), bf16)] * 3,
        LIMIT_B,
        "fold",
        kept, up_a, down_a, up_b, down_b,
    )
    mine, theirs, rates = local(
        split_kernel,
        [((half, SIDE // 2), f32), ((half, SIDE // 2), bf16), (rates.shape, f32)],
        LIMIT_B,
        "split",
        parts[0], *[send(parts[k], near(k)) for k in (2, 1, 3)], rates,
    )
    grads = [mine, send(theirs, partner)]

    state = (kv_weight.shape, f32)
    new_first, new_second, pseudo = local(
        inner_kernel,
        [state, state, (kv_weight.shape, bf16)],
        LIMIT_B,
        "inner_step",
        rates, first_moment[0], second_moment[0], kv_weight, *grads,
    )

    split = lax.all_to_all(pseudo.reshape(NZ, rows // NZ, columns), "island", 0, 0, tiled=True)
    share = jnp.sum(split.astype(f32), axis=0) / f32(NZ)
    spread = jnp.broadcast_to(share.astype(bf16)[None], (NZ, rows // NZ, columns))
    mean = lax.all_to_all(spread, "island", 0, 0, tiled=True).reshape(rows, columns).astype(f32)
    new_momentum = 0.9 * momentum + mean
    new_weight = kv_weight - 0.7 * (mean + 0.9 * new_momentum)
    return (new_weight, new_momentum, new_first[None], new_second[None])


def solution(mesh):
    placed = (
        P(("island", "fsdp", "dp"), None),
        P(("island", "fsdp", "dp"), None),
        P(("fsdp", "dp"), None),
        P(("fsdp", "dp"), None),
        P("island", ("fsdp", "dp"), None),
        P("island", ("fsdp", "dp"), None),
        P(),
    )
    return jax.shard_map(
        per_device,
        mesh=mesh,
        in_specs=placed,
        out_specs=(
            P(("fsdp", "dp"), None),
            P(("fsdp", "dp"), None),
            P("island", ("fsdp", "dp"), None),
            P("island", ("fsdp", "dp"), None),
        ),
        check_vma=False,
    )
```

```python
import functools
import jax
import jax.numpy as jnp
from jax import lax
from jax.experimental import pallas as pl
from jax.experimental.pallas import tpu as pltpu
from jax.sharding import PartitionSpec as P

WARM = 32
NX = NY = 4
NZ = 8
BIG = (768, 4096)
SIDE = 256
STEPS = 3
LOW, HIGH = (0, 1), (2, 3)
LIMIT_A = 10
LIMIT_B = 8
AXES = ("island", "fsdp", "dp")
MIB = 1024 * 1024
GIGA = 10**9
VM = pl.BlockSpec(memory_space=pltpu.VMEM)
SM = pl.BlockSpec(memory_space=pltpu.SMEM)


def flat(z, y, x, c):
    return (z % NZ) * 32 + (y % NY) * 8 + (x % NX) * 2 + c


def send(value, where):
    pairs = [
        (flat(z, y, x, c), flat(*where(z, y, x, c)))
        for z in range(NZ)
        for y in range(NY)
        for x in range(NX)
        for c in range(2)
    ]
    return lax.ppermute(value, AXES, pairs)


def near(k):
    return lambda z, y, x, c: (z, y, x + k, c) if c == 0 else (z, y + k, x, c)


def far(k):
    return lambda z, y, x, c: (z, y + k, x, c) if c == 0 else (z, y, x + k, c)


def partner(z, y, x, c):
    return (z, y, x, 1 - c)


def params(limit):
    return pltpu.CompilerParams(vmem_limit_bytes=limit * MIB)


def here():
    fsdp, dp = lax.axis_index("fsdp"), lax.axis_index("dp")
    return lax.div(fsdp, 2), lax.rem(fsdp, 2) * 2 + lax.div(dp, 2), lax.rem(dp, 2)


def chip(place, g, m):
    y, x, core = place
    outer = lax.rem(jnp.where(core == 0, y, x) + g, 4)
    inner = lax.rem(jnp.where(core == 0, x, y) + m, 4)
    return jnp.where(core == 0, outer * NX + inner, inner * NX + outer)


def columns_of(place, g, m):
    return pl.ds(pl.multiple_of(chip(place, g, m) * SIDE, SIDE), SIDE)


def term(place, g, m, s, so, x, xo):
    columns = columns_of(place, g, m)
    total = jnp.dot(s[...], x[:, columns], preferred_element_type=jnp.float32)
    return total + jnp.dot(so[...], xo[:, columns], preferred_element_type=jnp.float32)


def product(place, tokens, g, members, block, span=slice(None)):
    rows = [tokens[span, columns_of(place, g, m)] for m in members]
    return jnp.dot(jnp.concatenate(rows, axis=1), block, preferred_element_type=jnp.float32)


def first_kernel(a, b, c, d, x, xo, out, out_other, held, held_other, sems):
    place = here()
    rows = x.shape[0] // STEPS
    copies = []
    for i, (source, into) in enumerate(((x, held), (xo, held_other))):
        for k in range(STEPS):
            span = pl.ds(k * rows, rows)
            copies.append(pltpu.make_async_copy(source.at[span], into.at[span], sems.at[i, k]))
    for copy in copies:
        copy.start()
    block = jnp.concatenate([a[...], b[...], c[...], d[...]], axis=0)
    for i, (tokens, ref) in enumerate(((held, out), (held_other, out_other))):
        for k in range(STEPS):
            copies[i * STEPS + k].wait()
            span = slice(k * rows, (k + 1) * rows)
            ref[span, :] = product(place, tokens, 0, range(4), block, span).astype(ref.dtype)


def more_kernel(acc, acc_other, low_1, high_1, low_3, high_3, x, xo, out, out_other):
    place = here()
    blocks = ((1, (low_1, high_1)), (3, (low_3, high_3)))
    blocks = [(g, jnp.concatenate([ref[...] for ref in refs], axis=0)) for g, refs in blocks]
    for tokens, start, ref in ((x, acc, out), (xo, acc_other, out_other)):
        total = start[...].astype(jnp.float32)
        for g, block in blocks:
            total += product(place, tokens, g, range(4), block)
        ref[...] = total.astype(ref.dtype)


def stack_kernel(a, b, out):
    rows = a.shape[0]
    out[:rows, :] = a[...]
    out[rows:, :] = b[...]


def late_kernel(scales, acc, acc_other, va, vb, x, xo, to, t, s_ref, so_ref, relay_a, relay_b, aims, sem):
    place = here()
    fetch = pltpu.make_async_copy(t, aims, sem)
    fetch.start()
    inv_width, inv_count = scales
    for tokens, total, goals, out in ((xo, acc_other, to, so_ref), (x, acc, aims, s_ref)):
        proj = total[...].astype(jnp.float32) + product(place, tokens, 2, LOW, va[...]) + product(place, tokens, 2, HIGH, vb[...])
        if goals is aims:
            fetch.wait()
        scaled = (proj * inv_width - goals[...].astype(jnp.float32)) * inv_count
        out[...] = scaled.T.astype(jnp.bfloat16)
    for out, members in ((relay_a, LOW), (relay_b, HIGH)):
        for k, m in enumerate(members):
            out[:, k * SIDE : (k + 1) * SIDE] = term(place, 2, m, s_ref, so_ref, x, xo).astype(out.dtype)


def sides_kernel(members, s, so, x, xo, up, down):
    place = here()
    for g, out, chosen in ((1, up, members[0]), (3, down, members[1])):
        for k, m in enumerate(chosen):
            out[:, k * SIDE : (k + 1) * SIDE] = term(place, g, m, s, so, x, xo).astype(out.dtype)


def kept_kernel(s, so, x, xo, out):
    place = here()
    for m in range(4):
        out[:, m * SIDE : (m + 1) * SIDE] = term(place, 0, m, s, so, x, xo)


def fold_kernel(first, kept, up, down, *outs):
    for k, out in enumerate(outs):
        part = slice(k * SIDE, (k + 1) * SIDE)
        total = kept[:, (first + k) * SIDE : (first + k + 1) * SIDE]
        for ref in (up, down):
            total += ref[:, part].astype(jnp.float32)
        out[...] = total.astype(out.dtype)


def split_kernel(own, a, b, c, mine, theirs):
    total = own[...] + a[...].astype(jnp.float32) + b[...].astype(jnp.float32) + c[...].astype(jnp.float32)
    core = here()[2]
    low, high = total[:, : SIDE // 2], total[:, SIDE // 2 :]
    mine[...] = jnp.where(core == 0, low, high)
    theirs[...] = jnp.where(core == 0, high, low).astype(theirs.dtype)


def inner_kernel(rates, first, second, weight, *refs):
    grads, (new_first, new_second, pseudo) = refs[:-3], refs[-3:]
    core = here()[2]
    width = grads[0].shape[0]
    rate, first_scale, second_scale = rates[0:1, :], rates[1:2, :], rates[2:3, :]
    for k, ref in enumerate(grads):
        side = core if k % 2 == 0 else 1 - core
        columns = pl.ds(pl.multiple_of(side * width, width), width)
        grad = ref[...].astype(jnp.float32).T
        one = 0.9 * first[:, columns] + 0.1 * grad
        two = 0.95 * second[:, columns] + 0.05 * grad * grad
        update = (one * first_scale) / (jnp.sqrt(two * second_scale) + 1e-08)
        new_first[:, columns] = one
        new_second[:, columns] = two
        pseudo[:, columns] = (rate * (update + 0.1 * weight[:, columns])).astype(pseudo.dtype)


def local(kernel, shapes, limit, name, *operands, cost=1, alias={}):
    operands = [
        pltpu.with_memory_space_constraint(o, pltpu.VMEM) if o.shape == BIG else o for o in operands
    ]
    return pl.pallas_call(
        kernel,
        out_shape=[jax.ShapeDtypeStruct(*s) for s in shapes],
        in_specs=[VM] * len(operands),
        out_specs=[VM] * len(shapes),
        compiler_params=params(limit),
        input_output_aliases=alias,
        cost_estimate=pl.CostEstimate(flops=cost * GIGA, bytes_accessed=MIB, transcendentals=0),
        name=name,
    )(*operands)


def per_device(tokens, targets, kv_weight, momentum, first_moment, second_moment, step):
    f32, bf16 = jnp.float32, jnp.bfloat16
    count, features = tokens.shape
    rows, columns = kv_weight.shape
    half = columns // 2
    core = here()[2]
    scales = (1.0 / float(features) ** 0.5, 1.0 / float(count * 32) ** 0.5)

    whole = kv_weight.astype(bf16)
    own_half = lax.dynamic_slice_in_dim(whole, core * half, half, 1)
    other_half = lax.dynamic_slice_in_dim(whole, (1 - core) * half, half, 1)
    crossed = send(other_half, partner)
    crossed, tokens_now = lax.optimization_barrier((crossed, tokens))
    tokens_other = send(tokens_now, partner)
    shard = jnp.where(
        core == 0,
        jnp.concatenate([own_half, crossed], axis=0),
        jnp.concatenate([crossed, own_half], axis=0),
    )
    inner = [shard] + [send(shard, near(-k)) for k in (1, 2, 3)]
    tally = step.astype(f32)
    rate = 0.1 * jnp.minimum(tally, f32(WARM)) / f32(WARM)
    first_scale = 1.0 / (1.0 - jnp.power(f32(0.9), tally))
    second_scale = 1.0 / (1.0 - jnp.power(f32(0.95), tally))
    rates = jnp.stack([rate, first_scale, second_scale] + [rate] * 5)
    rates = jnp.broadcast_to(rates[:, None], (8, half))

    inner[3], targets = lax.optimization_barrier((inner[3], targets))
    goals = lax.dynamic_slice_in_dim(targets, core * half, half, 1)
    goals_other = lax.dynamic_slice_in_dim(targets, (1 - core) * half, half, 1)
    inner[2], goals, goals_other = lax.optimization_barrier((inner[2], goals, goals_other))
    goals_other = send(goals_other, partner)
    both = [((2 * inner[0].shape[0], half), bf16)]
    (high,) = local(stack_kernel, both, LIMIT_B, "stack", *inner[2:])
    (low,) = local(stack_kernel, both, LIMIT_B, "stack", *inner[:2])
    low, tokens_other = lax.optimization_barrier((low, tokens_other))
    low_1, high_3 = send(low, far(-1)), send(high, far(1))
    low_3 = send(low, far(1))
    high_1 = send(high, far(-1))
    low_2, high_2 = send(low_1, far(-1)), send(high_3, far(1))
    hbm = pl.BlockSpec(memory_space=pltpu.HBM)
    *acc, tokens, tokens_other = pl.pallas_call(
        first_kernel,
        out_shape=[jax.ShapeDtypeStruct((count, half), bf16)] * 2 + [pltpu.VMEM(tokens.shape, bf16)] * 2,
        in_specs=[VM] * 4 + [hbm] * 2,
        out_specs=[VM] * 4,
        scratch_shapes=[pltpu.SemaphoreType.DMA((2, STEPS))],
        compiler_params=params(LIMIT_A),
        name="first",
    )(
        *inner,
        pltpu.with_memory_space_constraint(tokens, pltpu.HBM),
        pltpu.with_memory_space_constraint(tokens_other, pltpu.HBM),
    )
    pair = (tokens, tokens_other)
    acc = local(
        more_kernel, [((count, half), bf16)] * 2, LIMIT_A, "more", *acc, low_1, high_1, low_3, high_3, *pair, cost=4
    )
    mid = ((half, 2 * SIDE), bf16)
    s, so, relay_a, relay_b = pl.pallas_call(
        functools.partial(late_kernel, scales),
        out_shape=[
            jax.ShapeDtypeStruct(*k) for k in [((half, count), bf16)] * 2 + [mid] * 2
        ],
        in_specs=[VM] * 7 + [hbm],
        out_specs=[VM] * 4,
        scratch_shapes=[pltpu.VMEM((count, half), bf16), pltpu.SemaphoreType.DMA],
        compiler_params=params(LIMIT_A),
        name="late",
    )(
        *acc,
        low_2, high_2,
        *[pltpu.with_memory_space_constraint(k, pltpu.VMEM) for k in pair],
        goals_other,
        pltpu.with_memory_space_constraint(goals, pltpu.HBM),
    )
    sides = functools.partial(sides_kernel, (HIGH, LOW))
    up_b, down_a = local(sides, [mid] * 2, LIMIT_B, "sides_near", s, so, *pair, cost=2)
    sides = functools.partial(sides_kernel, (LOW, HIGH))
    up_a, down_b = local(sides, [mid] * 2, LIMIT_B, "sides_rest", s, so, *pair, cost=2)
    (kept,) = local(kept_kernel, [((half, 4 * SIDE), f32)], LIMIT_B, "kept", s, so, *pair, cost=2)
    from_low, from_high = send(relay_a, far(1)), send(relay_b, far(-1))
    up_b, down_a = send(up_b, far(1)), send(down_a, far(-1))
    up_a = send((up_a.astype(f32) + from_low.astype(f32)).astype(bf16), far(1))
    down_b = send((down_b.astype(f32) + from_high.astype(f32)).astype(bf16), far(-1))
    part = (half, SIDE)
    fold = functools.partial(fold_kernel, 2)
    parts = local(fold, [(part, bf16)] * 2, LIMIT_B, "fold_high", kept, up_b, down_b)
    fold = functools.partial(fold_kernel, 0)
    parts = [*local(fold, [(part, f32), (part, bf16)], LIMIT_B, "fold_low", kept, up_a, down_a), *parts]
    mine, theirs = local(
        split_kernel,
        [((half, SIDE // 2), f32), ((half, SIDE // 2), bf16)],
        LIMIT_B,
        "split",
        parts[0], *[send(parts[k], near(k)) for k in (2, 1, 3)],
    )
    grads = [mine, send(theirs, partner)]

    state = (kv_weight.shape, f32)
    new_first, new_second, pseudo = local(
        inner_kernel,
        [state, state, (kv_weight.shape, bf16)],
        LIMIT_B,
        "inner_step",
        rates, first_moment[0], second_moment[0], kv_weight, *grads,
    )

    split = lax.all_to_all(pseudo.reshape(NZ, rows // NZ, columns), "island", 0, 0, tiled=True)
    share = jnp.sum(split.astype(f32), axis=0) / f32(NZ)
    spread = jnp.broadcast_to(share.astype(bf16)[None], (NZ, rows // NZ, columns))
    mean = lax.all_to_all(spread, "island", 0, 0, tiled=True).reshape(rows, columns).astype(f32)
    new_momentum = 0.9 * momentum + mean
    new_weight = kv_weight - 0.7 * (mean + 0.9 * new_momentum)
    return (new_weight, new_momentum, new_first[None], new_second[None])


def solution(mesh):
    placed = (
        P(("island", "fsdp", "dp"), None),
        P(("island", "fsdp", "dp"), None),
        P(("fsdp", "dp"), None),
        P(("fsdp", "dp"), None),
        P("island", ("fsdp", "dp"), None),
        P("island", ("fsdp", "dp"), None),
        P(),
    )
    return jax.shard_map(
        per_device,
        mesh=mesh,
        in_specs=placed,
        out_specs=(
            P(("fsdp", "dp"), None),
            P(("fsdp", "dp"), None),
            P("island", ("fsdp", "dp"), None),
            P("island", ("fsdp", "dp"), None),
        ),
        check_vma=False,
    )
```

```python
import functools
import jax
import jax.numpy as jnp
from jax import lax
from jax.experimental import pallas as pl
from jax.experimental.pallas import tpu as pltpu
from jax.sharding import PartitionSpec as P

WARM = 32
NX = NY = 4
NZ = 8
BIG = (768, 4096)
SIDE = 256
STEPS = 3
LOW, HIGH = (0, 1), (2, 3)
LIMIT_A = 10
LIMIT_B = 8
AXES = ("island", "fsdp", "dp")
MIB = 1024 * 1024
GIGA = 10**9
VM = pl.BlockSpec(memory_space=pltpu.VMEM)
SM = pl.BlockSpec(memory_space=pltpu.SMEM)


def flat(z, y, x, c):
    return (z % NZ) * 32 + (y % NY) * 8 + (x % NX) * 2 + c


def send(value, where):
    pairs = [
        (flat(z, y, x, c), flat(*where(z, y, x, c)))
        for z in range(NZ)
        for y in range(NY)
        for x in range(NX)
        for c in range(2)
    ]
    return lax.ppermute(value, AXES, pairs)


def near(k):
    return lambda z, y, x, c: (z, y, x + k, c) if c == 0 else (z, y + k, x, c)


def far(k):
    return lambda z, y, x, c: (z, y + k, x, c) if c == 0 else (z, y, x + k, c)


def partner(z, y, x, c):
    return (z, y, x, 1 - c)


def params(limit):
    return pltpu.CompilerParams(vmem_limit_bytes=limit * MIB)


def here():
    fsdp, dp = lax.axis_index("fsdp"), lax.axis_index("dp")
    return lax.div(fsdp, 2), lax.rem(fsdp, 2) * 2 + lax.div(dp, 2), lax.rem(dp, 2)


def chip(place, g, m):
    y, x, core = place
    outer = lax.rem(jnp.where(core == 0, y, x) + g, 4)
    inner = lax.rem(jnp.where(core == 0, x, y) + m, 4)
    return jnp.where(core == 0, outer * NX + inner, inner * NX + outer)


def columns_of(place, g, m):
    return pl.ds(pl.multiple_of(chip(place, g, m) * SIDE, SIDE), SIDE)


def term(place, g, m, s, so, x, xo):
    columns = columns_of(place, g, m)
    total = jnp.dot(s[...], x[:, columns], preferred_element_type=jnp.float32)
    return total + jnp.dot(so[...], xo[:, columns], preferred_element_type=jnp.float32)


def product(place, tokens, g, members, block, span=slice(None)):
    rows = [tokens[span, columns_of(place, g, m)] for m in members]
    return jnp.dot(jnp.concatenate(rows, axis=1), block, preferred_element_type=jnp.float32)


def first_kernel(a, b, c, d, x, xo, out, out_other, held, held_other, sems):
    place = here()
    rows = x.shape[0] // STEPS
    copies = []
    for i, (source, into) in enumerate(((x, held), (xo, held_other))):
        for k in range(STEPS):
            span = pl.ds(k * rows, rows)
            copies.append(pltpu.make_async_copy(source.at[span], into.at[span], sems.at[i, k]))
    for copy in copies:
        copy.start()
    block = jnp.concatenate([a[...], b[...], c[...], d[...]], axis=0)
    for i, (tokens, ref) in enumerate(((held, out), (held_other, out_other))):
        for k in range(STEPS):
            copies[i * STEPS + k].wait()
            span = slice(k * rows, (k + 1) * rows)
            ref[span, :] = product(place, tokens, 0, range(4), block, span).astype(ref.dtype)


def more_kernel(acc, acc_other, low_1, high_1, low_3, high_3, x, xo, t, out, out_other, goals, sem):
    place = here()
    half = goals.shape[1]
    columns = pl.ds(pl.multiple_of(place[2] * half, half), half)
    fetch = pltpu.make_async_copy(t.at[:, columns], goals, sem)
    fetch.start()
    blocks = ((1, (low_1, high_1)), (3, (low_3, high_3)))
    blocks = [(g, jnp.concatenate([ref[...] for ref in refs], axis=0)) for g, refs in blocks]
    for tokens, start, ref in ((x, acc, out), (xo, acc_other, out_other)):
        total = start[...].astype(jnp.float32)
        for g, block in blocks:
            total += product(place, tokens, g, range(4), block)
        ref[...] = total.astype(ref.dtype)
    fetch.wait()


def stack_kernel(a, b, out):
    rows = a.shape[0]
    out[:rows, :] = a[...]
    out[rows:, :] = b[...]


def late_kernel(scales, acc, acc_other, va, vb, x, xo, to, t, s_ref, so_ref, relay_a, relay_b):
    place = here()
    inv_width, inv_count = scales
    for tokens, total, goals, out in ((xo, acc_other, to, so_ref), (x, acc, t, s_ref)):
        proj = total[...].astype(jnp.float32) + product(place, tokens, 2, LOW, va[...]) + product(place, tokens, 2, HIGH, vb[...])
        scaled = (proj * inv_width - goals[...].astype(jnp.float32)) * inv_count
        out[...] = scaled.T.astype(jnp.bfloat16)
    for out, members in ((relay_a, LOW), (relay_b, HIGH)):
        for k, m in enumerate(members):
            out[:, k * SIDE : (k + 1) * SIDE] = term(place, 2, m, s_ref, so_ref, x, xo).astype(out.dtype)


def sides_kernel(members, s, so, x, xo, up, down):
    place = here()
    for g, out, chosen in ((1, up, members[0]), (3, down, members[1])):
        for k, m in enumerate(chosen):
            out[:, k * SIDE : (k + 1) * SIDE] = term(place, g, m, s, so, x, xo).astype(out.dtype)


def kept_kernel(s, so, x, xo, out):
    place = here()
    for m in range(4):
        out[:, m * SIDE : (m + 1) * SIDE] = term(place, 0, m, s, so, x, xo)


def fold_kernel(first, kept, up, down, *outs):
    for k, out in enumerate(outs):
        part = slice(k * SIDE, (k + 1) * SIDE)
        total = kept[:, (first + k) * SIDE : (first + k + 1) * SIDE]
        for ref in (up, down):
            total += ref[:, part].astype(jnp.float32)
        out[...] = total.astype(out.dtype)


def split_kernel(own, a, b, c, mine, theirs):
    total = own[...] + a[...].astype(jnp.float32) + b[...].astype(jnp.float32) + c[...].astype(jnp.float32)
    core = here()[2]
    low, high = total[:, : SIDE // 2], total[:, SIDE // 2 :]
    mine[...] = jnp.where(core == 0, low, high)
    theirs[...] = jnp.where(core == 0, high, low).astype(theirs.dtype)


def inner_kernel(rates, first, second, weight, *refs):
    grads, (new_first, new_second, pseudo) = refs[:-3], refs[-3:]
    core = here()[2]
    width = grads[0].shape[0]
    rate, first_scale, second_scale = rates[0:1, :], rates[1:2, :], rates[2:3, :]
    for k, ref in enumerate(grads):
        side = core if k % 2 == 0 else 1 - core
        columns = pl.ds(pl.multiple_of(side * width, width), width)
        grad = ref[...].astype(jnp.float32).T
        one = 0.9 * first[:, columns] + 0.1 * grad
        two = 0.95 * second[:, columns] + 0.05 * grad * grad
        update = (one * first_scale) / (jnp.sqrt(two * second_scale) + 1e-08)
        new_first[:, columns] = one
        new_second[:, columns] = two
        pseudo[:, columns] = (rate * (update + 0.1 * weight[:, columns])).astype(pseudo.dtype)


def local(kernel, shapes, limit, name, *operands, cost=1, alias={}):
    operands = [
        pltpu.with_memory_space_constraint(o, pltpu.VMEM) if o.shape == BIG else o for o in operands
    ]
    return pl.pallas_call(
        kernel,
        out_shape=[jax.ShapeDtypeStruct(*s) for s in shapes],
        in_specs=[VM] * len(operands),
        out_specs=[VM] * len(shapes),
        compiler_params=params(limit),
        input_output_aliases=alias,
        cost_estimate=pl.CostEstimate(flops=cost * GIGA, bytes_accessed=MIB, transcendentals=0),
        name=name,
    )(*operands)


def per_device(tokens, targets, kv_weight, momentum, first_moment, second_moment, step):
    f32, bf16 = jnp.float32, jnp.bfloat16
    count, features = tokens.shape
    rows, columns = kv_weight.shape
    half = columns // 2
    core = here()[2]
    scales = (1.0 / float(features) ** 0.5, 1.0 / float(count * 32) ** 0.5)

    whole = kv_weight.astype(bf16)
    own_half = lax.dynamic_slice_in_dim(whole, core * half, half, 1)
    other_half = lax.dynamic_slice_in_dim(whole, (1 - core) * half, half, 1)
    crossed = send(other_half, partner)
    crossed, tokens_now = lax.optimization_barrier((crossed, tokens))
    tokens_other = send(tokens_now, partner)
    shard = jnp.where(
        core == 0,
        jnp.concatenate([own_half, crossed], axis=0),
        jnp.concatenate([crossed, own_half], axis=0),
    )
    inner = [shard] + [send(shard, near(-k)) for k in (1, 2, 3)]
    tally = step.astype(f32)
    rate = 0.1 * jnp.minimum(tally, f32(WARM)) / f32(WARM)
    first_scale = 1.0 / (1.0 - jnp.power(f32(0.9), tally))
    second_scale = 1.0 / (1.0 - jnp.power(f32(0.95), tally))
    rates = jnp.stack([rate, first_scale, second_scale] + [rate] * 5)
    rates = jnp.broadcast_to(rates[:, None], (8, half))

    inner[3], goals = lax.optimization_barrier((inner[3], targets))
    goals_other = lax.dynamic_slice_in_dim(goals, (1 - core) * half, half, 1)
    inner[2], goals_other = lax.optimization_barrier((inner[2], goals_other))
    goals_other = send(goals_other, partner)
    both = [((2 * inner[0].shape[0], half), bf16)]
    (high,) = local(stack_kernel, both, LIMIT_B, "stack", *inner[2:])
    (low,) = local(stack_kernel, both, LIMIT_B, "stack", *inner[:2])
    low, tokens_other = lax.optimization_barrier((low, tokens_other))
    low_1, high_3 = send(low, far(-1)), send(high, far(1))
    low_3 = send(low, far(1))
    high_1 = send(high, far(-1))
    low_2, high_2 = send(low_1, far(-1)), send(high_3, far(1))
    hbm = pl.BlockSpec(memory_space=pltpu.HBM)
    *acc, tokens, tokens_other = pl.pallas_call(
        first_kernel,
        out_shape=[jax.ShapeDtypeStruct((count, half), bf16)] * 2 + [pltpu.VMEM(tokens.shape, bf16)] * 2,
        in_specs=[VM] * 4 + [hbm] * 2,
        out_specs=[VM] * 4,
        scratch_shapes=[pltpu.SemaphoreType.DMA((2, STEPS))],
        compiler_params=params(LIMIT_A),
        name="first",
    )(
        *inner,
        pltpu.with_memory_space_constraint(tokens, pltpu.HBM),
        pltpu.with_memory_space_constraint(tokens_other, pltpu.HBM),
    )
    pair = (tokens, tokens_other)
    *acc, goals = pl.pallas_call(
        more_kernel,
        out_shape=[jax.ShapeDtypeStruct((count, half), bf16)] * 3,
        in_specs=[VM] * 8 + [hbm],
        out_specs=[VM] * 3,
        scratch_shapes=[pltpu.SemaphoreType.DMA],
        compiler_params=params(LIMIT_A),
        cost_estimate=pl.CostEstimate(flops=4 * GIGA, bytes_accessed=MIB, transcendentals=0),
        name="more",
    )(
        *acc,
        low_1, high_1, low_3, high_3,
        *[pltpu.with_memory_space_constraint(k, pltpu.VMEM) for k in pair],
        pltpu.with_memory_space_constraint(targets, pltpu.HBM),
    )
    mid = ((half, 2 * SIDE), bf16)
    s, so, relay_a, relay_b = pl.pallas_call(
        functools.partial(late_kernel, scales),
        out_shape=[
            jax.ShapeDtypeStruct(*k) for k in [((half, count), bf16)] * 2 + [mid] * 2
        ],
        in_specs=[VM] * 8,
        out_specs=[VM] * 4,
        compiler_params=params(LIMIT_A),
        name="late",
    )(
        *acc,
        low_2, high_2,
        *[pltpu.with_memory_space_constraint(k, pltpu.VMEM) for k in pair],
        goals_other,
        goals,
    )
    sides = functools.partial(sides_kernel, (HIGH, LOW))
    up_b, down_a = local(sides, [mid] * 2, LIMIT_B, "sides_near", s, so, *pair, cost=2)
    sides = functools.partial(sides_kernel, (LOW, HIGH))
    up_a, down_b = local(sides, [mid] * 2, LIMIT_B, "sides_rest", s, so, *pair, cost=2)
    (kept,) = local(kept_kernel, [((half, 4 * SIDE), f32)], LIMIT_B, "kept", s, so, *pair, cost=2)
    from_low, from_high = send(relay_a, far(1)), send(relay_b, far(-1))
    up_b, down_a = send(up_b, far(1)), send(down_a, far(-1))
    up_a = send((up_a.astype(f32) + from_low.astype(f32)).astype(bf16), far(1))
    down_b = send((down_b.astype(f32) + from_high.astype(f32)).astype(bf16), far(-1))
    part = (half, SIDE)
    fold = functools.partial(fold_kernel, 2)
    parts = local(fold, [(part, bf16)] * 2, LIMIT_B, "fold_high", kept, up_b, down_b)
    fold = functools.partial(fold_kernel, 0)
    parts = [*local(fold, [(part, f32), (part, bf16)], LIMIT_B, "fold_low", kept, up_a, down_a), *parts]
    mine, theirs = local(
        split_kernel,
        [((half, SIDE // 2), f32), ((half, SIDE // 2), bf16)],
        LIMIT_B,
        "split",
        parts[0], *[send(parts[k], near(k)) for k in (2, 1, 3)],
    )
    grads = [mine, send(theirs, partner)]

    state = (kv_weight.shape, f32)
    new_first, new_second, pseudo = local(
        inner_kernel,
        [state, state, (kv_weight.shape, bf16)],
        LIMIT_B,
        "inner_step",
        rates, first_moment[0], second_moment[0], kv_weight, *grads,
    )

    split = lax.all_to_all(pseudo.reshape(NZ, rows // NZ, columns), "island", 0, 0, tiled=True)
    share = jnp.sum(split.astype(f32), axis=0) / f32(NZ)
    spread = jnp.broadcast_to(share.astype(bf16)[None], (NZ, rows // NZ, columns))
    mean = lax.all_to_all(spread, "island", 0, 0, tiled=True).reshape(rows, columns).astype(f32)
    new_momentum = 0.9 * momentum + mean
    new_weight = kv_weight - 0.7 * (mean + 0.9 * new_momentum)
    return (new_weight, new_momentum, new_first[None], new_second[None])


def solution(mesh):
    placed = (
        P(("island", "fsdp", "dp"), None),
        P(("island", "fsdp", "dp"), None),
        P(("fsdp", "dp"), None),
        P(("fsdp", "dp"), None),
        P("island", ("fsdp", "dp"), None),
        P("island", ("fsdp", "dp"), None),
        P(),
    )
    return jax.shard_map(
        per_device,
        mesh=mesh,
        in_specs=placed,
        out_specs=(
            P(("fsdp", "dp"), None),
            P(("fsdp", "dp"), None),
            P("island", ("fsdp", "dp"), None),
            P("island", ("fsdp", "dp"), None),
        ),
        check_vma=False,
    )
```
